512 devices in a mesh: var: 128 (over x, z, core), samp: 4 (over y).
Axes of the slice: x: 4, y: 4, z: 16, core: 2. Of those that a mesh axis runs over, the one named last changes fastest.
Arguments:
- data: bfloat16 [128, 131072], P('samp', 'var'), may hold values from -6 to 6
- omega: float32 [8192, 128, 128], P(('var', 'samp')), may hold values from -0.3 to 2.3, as said below
- tile_row: int32 [128, 64], P('var'), may hold values from 0 to 7, as said below
- tile_col: int32 [128, 64], P('var'), may hold values from 0 to 1023, as said below
- tile_count: int32 [128], P('var'), may hold values from 60 to 64, as said below
- tile_active: int32 [128, 64], P('var'), may hold values 0 or 1
Outputs:
- omega_next: float32 [8192, 128, 128], P(('var', 'samp'))
The draws below stay inside these ranges and needn't reach their ends.
Inputs may be any that keep to these rules, and one draw needn't show every extreme that they name: `tile_row`: entries 0 to 7 of a block row have tile rows 0 to 7 in order; the others name any tile row of the block row. `tile_col`: entry k < 8 of block row r is column tile r * 8 + k. Every other entry names a column tile of another block row; no column tile twice in a block row, and at most 1 column tiles from any one other block row, a bound that some block row reaches. `tile_count`: some block row lists all 64 entries. `omega`: on entries k < 8 the diagonal of each tile lies between 0.7 and 2.3.
All inputs are finite; a program needn't handle non-finite values. No bound on the sum of `tile_active` on one device may be relied on, other than what follows from the above.
Results may differ from the reference program's by a relative error of at most 0.02.
Values may be sent and summed in bfloat16 or wider, within the bound.
A program may use at most 128 MiB of HBM per device.

```python
import jax
import jax.numpy as jnp
from jax import lax

TILE = 128
TR = 8
KMAX = 64
NS = 32
NSAMP = 128
P_SIZE = 131072
N_VAR = 128
N_SAMP = 4


def draw_omega(key, part):
    key = jax.random.fold_in(key, 11)
    first, second = jax.random.split(key)
    spread = jax.random.truncated_normal(first, -6.0, 6.0, (N_VAR * KMAX, TILE, TILE), jnp.float32) * 0.05
    diagonal = jax.random.uniform(second, (N_VAR * KMAX, TILE), jnp.float32, 1.0, 2.0)
    entries = jnp.arange(N_VAR * KMAX) % KMAX
    identity = jnp.eye(TILE, dtype=jnp.float32)
    boost = jnp.where((entries < TR)[:, None, None], identity[None, :, :] * diagonal[:, None, :], 0.0)
    return spread + boost


def draw_tile_row(key, part):
    key = jax.random.fold_in(key, 12)
    picked = jax.random.randint(key, (N_VAR, KMAX), 0, TR, jnp.int32)
    entries = jnp.arange(KMAX, dtype=jnp.int32)[None, :]
    return jnp.where(entries < TR, entries, picked).astype(jnp.int32)


def draw_tile_col(key, part):
    key = jax.random.fold_in(key, 13)
    first, second, third = jax.random.split(key, 3)
    popular = (jax.random.randint(first, (N_VAR,), 0, 4, jnp.int32) == 0).astype(jnp.int32)
    offsets = jnp.arange(N_VAR - 1, dtype=jnp.int32)
    owner_ids = jnp.arange(N_VAR, dtype=jnp.int32)
    peer_of = (owner_ids[:, None] + 1 + offsets[None, :]) % N_VAR
    base_score = jax.random.randint(second, (N_VAR, N_VAR - 1), 0, 4096, jnp.int32)
    scores = (base_score + popular[peer_of] * 2048) * N_VAR + offsets[None, :]
    ranking = lax.top_k(scores, N_VAR - 1)[1].astype(jnp.int32)
    remote_entries = jnp.arange(KMAX - TR, dtype=jnp.int32)
    position = remote_entries % (N_VAR - 1)
    copy_index = remote_entries // (N_VAR - 1)
    chosen = ranking[:, position]
    peer_owner = (owner_ids[:, None] + 1 + chosen) % N_VAR
    rotation = jax.random.randint(third, (N_VAR, N_VAR - 1), 0, TR, jnp.int32)
    local_tile = (jnp.take_along_axis(rotation, chosen, axis=1) + copy_index[None, :]) % TR
    remote_cols = peer_owner * TR + local_tile
    diag_cols = owner_ids[:, None] * TR + jnp.arange(TR, dtype=jnp.int32)[None, :]
    return jnp.concatenate([diag_cols, remote_cols], axis=1).astype(jnp.int32)


def draw_tile_count(key, part):
    key = jax.random.fold_in(key, 14)
    first, second = jax.random.split(key)
    dropped = jax.random.randint(first, (N_VAR,), 0, 5, jnp.int32)
    full_owner = jax.random.randint(second, (), 0, N_VAR, jnp.int32)
    owner_ids = jnp.arange(N_VAR, dtype=jnp.int32)
    return (KMAX - jnp.where(owner_ids == full_owner, 0, dropped)).astype(jnp.int32)


def plant(drawn, stream_key, smallest, largest):
    shape = drawn.shape
    place = [jax.random.randint(jax.random.fold_in(stream_key, axis), (), 0, shape[axis]) for axis in range(len(shape))]
    drawn = drawn.at[tuple(place)].set(smallest)
    longest = shape.index(max(shape))
    place[longest] = (place[longest] + 1) % shape[longest]
    return drawn.at[tuple(place)].set(largest)


def block_levels(key, extent, pieces, low, top_value):
    def one(axis_at, blocks):
        draws = jax.random.uniform(jax.random.fold_in(jax.random.fold_in(key, 6), axis_at), (blocks,), jnp.float32, low / len(pieces), top_value / len(pieces))
        return jnp.repeat(jnp.exp(draws), extent[axis_at] // blocks).reshape((-1,) + (1,) * (len(extent) - axis_at - 1))

    gain = one(*pieces[0])
    for cut in pieces[1:]:
        gain = gain * one(*cut)
    return gain


def normal_values(rng, extent, deviation, most, shards=(), kind=jnp.bfloat16):
    gain = block_levels(rng, extent, shards, -0.22, 0.18) if shards else 1.0
    values = jax.random.normal(rng, extent, jnp.float32) * deviation * gain
    return jnp.minimum(jnp.maximum(values, -most), most).astype(kind)


def setup_inputs(seed: int = 0) -> dict:
    arg_keys = jax.random.split(jax.random.key(seed), 7)
    return {
        "data": normal_values(arg_keys[0], (NSAMP, P_SIZE), 1.0, 6.0, ((0, 4), (1, 128))),
        "omega": draw_omega(jax.random.fold_in(arg_keys[6], 71), 0),
        "tile_row": draw_tile_row(jax.random.fold_in(arg_keys[6], 71), 0),
        "tile_col": draw_tile_col(jax.random.fold_in(arg_keys[6], 71), 0),
        "tile_count": draw_tile_count(jax.random.fold_in(arg_keys[6], 71), 0),
        "tile_active": plant((jax.random.randint(arg_keys[5], (N_VAR, KMAX), 0, 4) < 3).astype(jnp.int32), jax.random.fold_in(arg_keys[5], 1), 0, 1),
    }


step_size = 1.0
penalty = 0.05


def reference(data, omega, tile_row, tile_col, tile_count, tile_active):
    data_tiles = data.reshape(NSAMP, N_VAR * TR, TILE)
    omega_blocks = omega.reshape(N_VAR, KMAX, TILE, TILE)
    entries = jnp.arange(KMAX, dtype=jnp.int32)
    tile_range = jnp.arange(TR, dtype=jnp.int32)

    def image_block(inputs):
        tiles, rows_here, columns, count = inputs
        is_live = entries < count
        col_data = jnp.take(data_tiles, columns, axis=1).astype(jnp.float32)
        low_tiles = lax.optimization_barrier(tiles.astype(jnp.bfloat16)).astype(jnp.float32)
        products = jnp.einsum('skt,kut->sku', col_data, low_tiles)
        weights = ((rows_here[:, None] == tile_range[None, :]) & is_live[:, None]).astype(jnp.float32)
        return jnp.einsum('sku,kr->sru', products, weights).astype(jnp.bfloat16)

    image = lax.map(image_block, (omega_blocks, tile_row, tile_col, tile_count))
    image_tiles = jnp.transpose(image, (1, 0, 2, 3)).reshape(NSAMP, N_VAR * TR, TILE)
    identity = jnp.eye(TILE, dtype=jnp.float32)
    owners = jnp.arange(N_VAR, dtype=jnp.int32)

    def update_block(inputs):
        tiles, rows_here, columns, count, active, owner = inputs
        is_live = entries < count
        is_diag = entries < TR
        global_rows = (owner * TR + rows_here).astype(jnp.int32)
        row_data = jnp.take(data_tiles, global_rows, axis=1).astype(jnp.float32)
        row_image = jnp.take(image_tiles, global_rows, axis=1).astype(jnp.float32)
        col_data = jnp.take(data_tiles, columns, axis=1).astype(jnp.float32)
        col_image = jnp.take(image_tiles, columns, axis=1).astype(jnp.float32)
        gradient = jnp.zeros((KMAX, TILE, TILE), jnp.float32)
        for shard in range(N_SAMP):
            lower = shard * NS
            term = jnp.einsum('sku,skt->kut', row_image[lower:lower + NS], col_data[lower:lower + NS])
            term = term + jnp.einsum('sku,skt->kut', row_data[lower:lower + NS], col_image[lower:lower + NS])
            term = term * (0.5 / NSAMP)
            term = lax.optimization_barrier(term.astype(jnp.bfloat16)).astype(jnp.float32)
            gradient = gradient + term
        diagonal = jnp.diagonal(tiles, axis1=1, axis2=2)
        safe_diag = jnp.where(is_diag[:, None], diagonal, 1.0)
        gradient = gradient - jnp.where(is_diag[:, None, None], identity[None, :, :] / safe_diag[:, None, :], 0.0)
        stepped = tiles - step_size * gradient
        shrunk = jnp.sign(stepped) * jnp.maximum(jnp.abs(stepped) - step_size * penalty, 0.0)
        on_diag = is_diag[:, None, None] & (identity[None, :, :] > 0.5)
        proximal = jnp.where(on_diag, stepped, shrunk)
        held = jnp.where(active[:, None, None] > 0, proximal, tiles)
        return jnp.where(is_live[:, None, None], held, 0.0)

    result = lax.map(update_block, (omega_blocks, tile_row, tile_col, tile_count, tile_active, owners))
    return result.reshape(N_VAR * KMAX, TILE, TILE)
```

```python
import jax
import jax.numpy as jnp
from jax import lax
from jax.experimental import pallas as pl
from jax.experimental.pallas import tpu as pltpu
from jax.sharding import PartitionSpec as P

penalty = 0.05

NX, NZ, NC, NY = 4, 16, 2, 4
GROUPS = NX * NC
HALF = NZ // 2
TILE = 128
TR = 8
KMAX = 64
NS = 32
SHARE = KMAX // NY
NSAMP = NS * NY
MESH = pl.DeviceIdType.MESH
BF = jnp.bfloat16


def kernel(
    data_ref, omega_ref, cols_ref, row_s, col_s, count_s, active_s, out_ref,
    *scratch,
):
    scratch = list(scratch)

    def take(n):
        got = scratch[:n]
        del scratch[:n]
        return got

    zbufs = [take(NZ), take(NZ)]
    stages = take(2)
    places = take(2)
    omega_all, lhs, picked, picked_image, rhs, rows, rows_t = take(7)
    want_v, want_s, slot_v, slot_s = take(4)
    zsend, zrecv, xsend, xrecv = take(4)
    wsend, wrecv, lsem = take(3)
    osend, orecv, ysend, yrecv = take(4)

    var = lax.axis_index("var")
    y = lax.axis_index("samp")
    x = var // (NZ * NC)
    z = lax.rem(var // NC, NZ)
    c = lax.rem(var, NC)

    def at(dx=0, dz=0, dc=0, dy=0):
        to = (lax.rem(x + dx, NX) * NZ + lax.rem(z + dz, NZ)) * NC + lax.rem(c + dc, NC)
        return (to, lax.rem(y + dy, NY))

    def remote(src, dst, send, recv, to):
        return pltpu.make_async_remote_copy(
            src_ref=src, dst_ref=dst, send_sem=send, recv_sem=recv, device_id=to, device_id_type=MESH
        )

    barrier = pltpu.get_barrier_semaphore()
    partners = [at(dz=1), at(dz=NZ - 1)]
    partners += [at(dx=g // NC, dc=g % NC) for g in range(1, GROUPS)]
    partners += [at(dy=d) for d in range(1, NY)]
    for to in partners:
        pl.semaphore_signal(barrier, inc=1, device_id=to, device_id_type=MESH)

    count = count_s[0]
    for t in range(TR):
        zbufs[0][0][t] = data_ref[:, t * TILE:(t + 1) * TILE]

    lane = lax.broadcasted_iota(jnp.int32, (1, TILE), 1)

    def want(k, held):
        col = col_s[0, k]
        owner = jnp.where(k < count, col // TR, -1)
        return jnp.where(lane == owner, lax.rem(col, TR), held)

    want_v[0] = lax.fori_loop(TR, KMAX, want, jnp.zeros((1, TILE), jnp.int32))

    cols = cols_ref[...]
    owner = cols // TR
    dx = lax.rem(owner // (NZ * NC) - x + NX, NX)
    dz = lax.rem(lax.rem(owner // NC, NZ) - z + NZ, NZ)
    dc = lax.rem(lax.rem(owner, NC) + c, NC)
    order = jnp.where(
        dz == 0, 0, jnp.where(dz < HALF, 2 * dz - 1, jnp.where(dz == HALF, NZ - 1, 2 * (NZ - dz)))
    )
    slot_v[...] = (dx * NC + dc) * NZ + order

    pl.semaphore_wait(barrier, len(partners))

    def zcopy(phase, side, step):
        bufs = zbufs[phase]
        src = bufs[0] if step == 1 else bufs[(step - 1) + side * HALF]
        dst = bufs[HALF] if step == HALF else bufs[step + side * HALF]
        if step == HALF:
            part = pl.ds(side * (TR // 2), TR // 2)
            src, dst = src.at[part], dst.at[part]
        index = side * HALF + step - 1
        return remote(
            src, dst, zsend.at[phase, index], zrecv.at[phase, index], at(dz=NZ - 1 if side else 1)
        )

    def select(phase, step):
        bufs, stage, place = zbufs[phase], stages[phase], places[phase]
        if step == 0:
            pieces, first = [(bufs[0], 0)], 0
        elif step < HALF:
            pieces, first = [(bufs[step + HALF], step), (bufs[step], NZ - step)], 2 * step - 1
        else:
            pieces, first = [(bufs[HALF], HALF)], NZ - 1

        def tile(g, buf, dz):
            wanted = want_s[g, 0, (x * NZ + lax.rem(z + dz, NZ)) * NC + c]
            return buf[wanted]

        def send(g, carry):
            for j, (buf, dz) in enumerate(pieces):
                stage[(g - 1) * NZ + first + j] = tile(g, buf, dz)
            dx, dc = g // NC, lax.rem(g, NC)
            there = lax.rem(NX - dx, NX) * NC + dc
            remote(
                stage.at[pl.ds((g - 1) * NZ + first, len(pieces))],
                place.at[pl.ds(there * NZ + first, len(pieces))],
                xsend.at[phase],
                xrecv.at[phase],
                at(dx=dx, dc=dc),
            ).start()
            return carry

        lax.fori_loop(1, GROUPS, send, 0)
        for j, (buf, dz) in enumerate(pieces):
            place[first + j] = tile(0, buf, dz)

    def gather(phase, hooks):
        for side in (0, 1):
            zcopy(phase, side, 1).start()
        if 0 in hooks:
            hooks[0]()
        select(phase, 0)
        for step in range(1, HALF + 1):
            for side in (0, 1):
                zcopy(phase, side, step).wait_recv()
                if step < HALF:
                    zcopy(phase, side, step + 1).start()
            select(phase, step)
            if step in hooks:
                hooks[step]()
        wait_all(phase).wait_recv()

    def wait_all(phase):
        count = (GROUPS - 1) * NZ
        return remote(
            stages[phase], places[phase].at[pl.ds(NZ, count)], xsend.at[phase], xrecv.at[phase], at(dx=1)
        )

    HALF_ROWS = SHARE * TILE // 2

    def ocopy(side, hop, half):
        owner = y if hop == 0 else lax.rem(y + (NY - 1 if side == 0 else 1), NY)
        part = omega_all.at[pl.ds(pl.multiple_of(owner * (2 * HALF_ROWS) + half * HALF_ROWS, HALF_ROWS), HALF_ROWS)]
        index = side * 3 + (2 if hop else half)
        return remote(part, part, osend.at[index], orecv.at[index], at(dy=1 if side == 0 else NY - 1))

    def wcopy(g):
        dx, dc = g // NC, g % NC
        there = ((NX - dx) % NX) * NC + dc
        return remote(want_v.at[0], want_v.at[there], wsend, wrecv, at(dx=dx, dc=dc))

    def start_hook():
        for g in range(1, GROUPS):
            wcopy(g).start()

        def cast(e, carry):
            low = omega_ref[e].astype(BF)
            omega_all[pl.ds(pl.multiple_of((y * SHARE + e) * TILE, TILE), TILE)] = low.T
            return carry

        lax.fori_loop(0, SHARE, cast, 0)
        for half in (0, 1):
            ocopy(0, 0, half).start()
            ocopy(1, 0, 1 - half).start()
        remote(want_v.at[pl.ds(1, GROUPS - 1)], want_v.at[pl.ds(1, GROUPS - 1)], wsend, wrecv, at(dx=1)).wait_recv()
        one = pltpu.make_async_copy(want_v, want_s, lsem.at[0])
        two = pltpu.make_async_copy(slot_v, slot_s, lsem.at[1])
        one.start()
        two.start()
        one.wait()
        two.wait()

    def forward_hook():
        ocopy(0, 0, 0).wait_recv()
        ocopy(0, 1, 0).start()
        ocopy(1, 0, 1).wait_recv()
        ocopy(1, 1, 1).start()

    gather(0, {0: start_hook, 4: forward_hook})

    own, place = zbufs[0][0], places[0]

    def put(k, tile):
        picked[k] = tile
        row = jnp.where(k < count, row_s[0, k], TR)
        for r in range(TR):
            lhs[r * NS:(r + 1) * NS, pl.ds(pl.multiple_of(k * TILE, TILE), TILE)] = jnp.where(
                row == r, tile, jnp.zeros_like(tile)
            )

    def put_own(k, carry):
        put(k, own[k])
        return carry

    def put_other(k, carry):
        put(k, place[slot_s[0, k]])
        return carry

    lax.fori_loop(0, TR, put_own, 0)
    lax.fori_loop(TR, KMAX, put_other, 0)

    def ycopy(kind, d):
        to = lax.rem(y + d, NY)
        here = pl.ds(pl.multiple_of(y * NS, NS), NS)
        there = pl.ds(pl.multiple_of(NSAMP + y * NS, NS), NS)
        mine = pl.ds(to * SHARE, SHARE)
        src, dst = (
            (picked.at[mine], rhs.at[:, here]),
            (zbufs[0][0], rows.at[:, there]),
            (zbufs[1][0], rows.at[:, here]),
            (picked_image.at[mine], rhs.at[:, there]),
        )[kind]
        return remote(src, dst, ysend.at[kind, d - 1], yrecv.at[kind, d - 1], at(dy=d))

    for side in (0, 1):
        ocopy(side, 0, 1 - side).wait_recv()
        ocopy(side, 1, side).wait_recv()

    CHUNK = 8 * TILE

    def multiply(i, total):
        part = pl.ds(pl.multiple_of(i * CHUNK, CHUNK), CHUNK)
        return total + jnp.dot(lhs[:, part], omega_all[part], preferred_element_type=jnp.float32)

    total = lax.fori_loop(0, KMAX * TILE // CHUNK, multiply, jnp.zeros((TR * NS, TILE), jnp.float32))
    image = total.astype(BF)
    for r in range(TR):
        zbufs[1][0][r] = image[r * NS:(r + 1) * NS]

    def y_hook():
        for kind in (0, 1, 2):
            for d in (1, 3, 2):
                ycopy(kind, d).start()

    gather(1, {0: y_hook})

    place = places[1]

    def image_own(k, carry):
        picked_image[k] = zbufs[1][0][k]
        return carry

    def image_other(k, carry):
        picked_image[k] = place[slot_s[0, k]]
        return carry

    lax.fori_loop(0, TR, image_own, 0)
    lax.fori_loop(TR, KMAX, image_other, 0)
    for d in (2, 1, 3):
        ycopy(3, d).start()

    here = pl.ds(pl.multiple_of(y * NS, NS), NS)
    there = pl.ds(pl.multiple_of(NSAMP + y * NS, NS), NS)
    for r in range(TR):
        rows[r, here] = zbufs[1][0][r]
        rows[r, there] = zbufs[0][0][r]

    def keep(e, carry):
        rhs[e, here] = picked[y * SHARE + e]
        rhs[e, there] = picked_image[y * SHARE + e]
        return carry

    lax.fori_loop(0, SHARE, keep, 0)
    for kind in (1, 2):
        for d in range(1, NY):
            ycopy(kind, d).wait_recv()
    for r in range(TR):
        rows_t[r] = rows[r].T
    for kind in (0, 3):
        for d in range(1, NY):
            ycopy(kind, d).wait_recv()

    eye = lax.broadcasted_iota(jnp.int32, (TILE, TILE), 0) == lax.broadcasted_iota(
        jnp.int32, (TILE, TILE), 1
    )

    def update(e, carry):
        k = y * SHARE + e
        gradient = jnp.dot(rows_t[row_s[0, k]], rhs[e], preferred_element_type=jnp.float32) * (0.5 / NSAMP)
        omega = omega_ref[e]
        on_diag = eye & (k < TR)
        gradient = gradient - jnp.where(on_diag, 1.0 / jnp.where(on_diag, omega, 1.0), 0.0)
        stepped = omega - gradient
        shrunk = stepped - jnp.minimum(jnp.maximum(stepped, -penalty), penalty)
        proximal = jnp.where(on_diag, stepped, shrunk)
        held = jnp.where(active_s[0, k] > 0, proximal, omega)
        out_ref[e] = jnp.where(k < count, held, 0.0)
        return carry

    lax.fori_loop(0, SHARE, update, 0)

    for phase in (0, 1):
        for side in (0, 1):
            for step in range(1, HALF + 1):
                zcopy(phase, side, step).wait_send()
        wait_all(phase).wait_send()
    remote(want_v.at[pl.ds(1, GROUPS - 1)], want_v.at[pl.ds(1, GROUPS - 1)], wsend, wrecv, at(dx=1)).wait_send()
    for side in (0, 1):
        for half in (0, 1):
            ocopy(side, 0, half).wait_send()
        ocopy(side, 1, side).wait_send()
    for kind in range(4):
        for d in range(1, NY):
            ycopy(kind, d).wait_send()


def local(data, omega, tile_row, tile_col, tile_count, tile_active):
    vmem = pl.BlockSpec(memory_space=pltpu.VMEM)
    smem = pl.BlockSpec(memory_space=pltpu.SMEM)
    block = pltpu.VMEM((TR, NS, TILE), BF)
    scratch = [block] * (2 * NZ)
    scratch += [pltpu.VMEM(((GROUPS - 1) * NZ, NS, TILE), BF)] * 2
    scratch += [pltpu.VMEM((GROUPS * NZ, NS, TILE), BF)] * 2
    scratch += [
        pltpu.VMEM((KMAX * TILE, TILE), BF),
        pltpu.VMEM((TR * NS, KMAX * TILE), BF),
        pltpu.VMEM((KMAX, NS, TILE), BF),
        pltpu.VMEM((KMAX, NS, TILE), BF),
        pltpu.VMEM((SHARE, 2 * NSAMP, TILE), BF),
        pltpu.VMEM((TR, 2 * NSAMP, TILE), BF),
        pltpu.VMEM((TR, TILE, 2 * NSAMP), BF),
        pltpu.VMEM((GROUPS, 1, TILE), jnp.int32),
        pltpu.SMEM((GROUPS, 1, TILE), jnp.int32),
        pltpu.VMEM((1, KMAX), jnp.int32),
        pltpu.SMEM((1, KMAX), jnp.int32),
    ]
    dma = pltpu.SemaphoreType.DMA
    scratch += [dma((2, NZ)), dma((2, NZ)), dma((2,)), dma((2,))]
    scratch += [dma, dma, dma((2,))]
    scratch += [dma((6,)), dma((6,)), dma((4, NY - 1)), dma((4, NY - 1))]
    return pl.pallas_call(
        kernel,
        out_shape=jax.ShapeDtypeStruct(omega.shape, omega.dtype),
        in_specs=[vmem, vmem, vmem, smem, smem, smem, smem],
        out_specs=vmem,
        scratch_shapes=scratch,
        compiler_params=pltpu.CompilerParams(
            collective_id=0, has_side_effects=True, vmem_limit_bytes=40 * 2**20
        ),
    )(data, omega, tile_col, tile_row, tile_col, tile_count, tile_active)


def solution(mesh):
    placed = (
        P("samp", "var"),
        P(("var", "samp"), None, None),
        P("var", None),
        P("var", None),
        P("var"),
        P("var", None),
    )
    return jax.shard_map(
        local, mesh=mesh, in_specs=placed, out_specs=P(("var", "samp"), None, None), check_vma=False
    )
```

```python
import jax
import jax.numpy as jnp
from jax import lax
from jax.experimental import pallas as pl
from jax.experimental.pallas import tpu as pltpu
from jax.sharding import PartitionSpec as P

penalty = 0.05

NX, NZ, NC, NY = 4, 16, 2, 4
STRIDE = 3
CHUNKS = 5
PLANE = NX * NC
GROUPS = PLANE * STRIDE
LOCAL = 1 + CHUNKS
SLOTS = GROUPS * CHUNKS + PLANE
TILE = 128
TR = 8
KMAX = 64
NS = 32
SHARE = KMAX // NY
NSAMP = NS * NY
MESH = pl.DeviceIdType.MESH
BF = jnp.bfloat16


def split(g):
    i = g % STRIDE
    return g // (NC * STRIDE), (0, 1, NZ - 1)[i], (g // STRIDE) % NC


def mirrored(g):
    dx, dc, i = g // (NC * STRIDE), (g // STRIDE) % NC, g % STRIDE
    return (((NX - dx) % NX) * NC + dc) * STRIDE + (STRIDE - i) % STRIDE


def kernel(
    data_hbm, omega_hbm, cols_ref, row_s, col_s, count_s, active_s, out_ref,
    *scratch,
):
    scratch = list(scratch)

    def take(n):
        got = scratch[:n]
        del scratch[:n]
        return got

    zbufs = [take(CHUNKS + 1), take(CHUNKS + 1)]
    stages = take(2)
    places = take(2)
    data_ref, omega_ref = take(2)
    omega_all, lhs, picked, picked_image, rhs, rows, rows_t = take(7)
    want_v, want_s, slot_v, slot_s = take(4)
    zsend, zrecv, xsend, xrecv = take(4)
    wsend, wrecv, lsem = take(3)
    osend, orecv, ysend, yrecv = take(4)

    load_data = pltpu.make_async_copy(data_hbm, data_ref, lsem.at[2])
    load_omega = pltpu.make_async_copy(omega_hbm, omega_ref, lsem.at[3])
    load_data.start()
    load_omega.start()

    var = lax.axis_index("var")
    y = lax.axis_index("samp")
    x = var // (NZ * NC)
    z = lax.rem(var // NC, NZ)
    c = lax.rem(var, NC)

    xs = [x] + [lax.rem(x + d, NX) for d in range(1, NX)]
    zs = [z] + [lax.rem(z + d, NZ) for d in range(1, NZ)]
    cs = [c, 1 - c]
    ys = [y] + [lax.rem(y + d, NY) for d in range(1, NY)]

    def at(dx=0, dz=0, dc=0, dy=0):
        return ((xs[dx] * NZ + zs[dz % NZ]) * NC + cs[dc], ys[dy])

    def served(g):
        dx, dz, dc = split(g)
        return at(dx=dx, dz=dz, dc=dc)

    def remote(src, dst, send, recv, to):
        return pltpu.make_async_remote_copy(
            src_ref=src, dst_ref=dst, send_sem=send, recv_sem=recv, device_id=to, device_id_type=MESH
        )

    barrier = pltpu.get_barrier_semaphore()
    partners = [served(g) for g in range(1, GROUPS)]
    partners += [at(dz=dz) for dz in (STRIDE, NZ - STRIDE, 2, NZ - 2)]
    partners += [at(dy=d) for d in range(1, NY)]
    for to in partners:
        pl.semaphore_signal(barrier, inc=1, device_id=to, device_id_type=MESH)

    count = count_s[0]

    lane = lax.broadcasted_iota(jnp.int32, (1, TILE), 1)

    def want(k, held):
        col = col_s[0, k]
        owner = jnp.where(k < count, col // TR, -1)
        return jnp.where(lane == owner, lax.rem(col, TR), held)

    want_v[0] = lax.fori_loop(TR, KMAX, want, jnp.zeros((1, TILE), jnp.int32))

    cols = cols_ref[...]
    owner = cols // TR
    dx = lax.rem(owner // (NZ * NC) - x + NX, NX)
    dz = lax.rem(lax.rem(owner // NC, NZ) - z + NZ, NZ)
    dc = lax.rem(lax.rem(owner, NC) + c, NC)
    opposite = dz == NZ // 2
    step = lax.rem(dz + NZ // 2 - 1, NZ)
    side = lax.rem(step, STRIDE)
    far = step // STRIDE
    side = jnp.where(side == 0, 2, side - 1)
    far = jnp.where(far == 2, 0, jnp.where(far == 3, 1, jnp.where(far == 1, 2, jnp.where(far == 4, 3, 4))))
    plane = dx * NC + dc
    slot_v[...] = jnp.where(
        opposite,
        jnp.where(plane == 0, 0, SLOTS - PLANE + plane),
        1 + (plane * STRIDE + side) * CHUNKS + far,
    )

    load_data.wait()
    for t in range(TR):
        zbufs[0][0][t] = data_ref[:, t * TILE:(t + 1) * TILE]

    pl.semaphore_wait(barrier, len(partners))

    PLACES = (0, STRIDE, NZ - STRIDE, 2 * STRIDE, NZ - 2 * STRIDE, NZ // 2)

    def zcopy(phase, j):
        bufs = zbufs[phase]
        src, dst = bufs[max(j - 2, 0)], bufs[min(j, CHUNKS)]
        dz = STRIDE if j <= 4 else 2
        if j > 4:
            part = pl.ds((j - 5) * (TR // 2), TR // 2)
            src, dst = src.at[part], dst.at[part]
        return remote(
            src, dst, zsend.at[phase, j - 1], zrecv.at[phase, j - 1], at(dz=NZ - dz if j % 2 else dz)
        )

    def select(phase, first, number):
        bufs, stage, place = zbufs[phase], stages[phase], places[phase]
        pieces = range(first, first + number)
        last = first == CHUNKS

        def tile(g, j):
            return bufs[j][want_s[g, 0, at(dz=PLACES[j])[0]]]

        for g in range(STRIDE if last else 1, GROUPS, STRIDE if last else 1):
            if last:
                here = GROUPS * CHUNKS - LOCAL + g // STRIDE
                there = GROUPS * CHUNKS + mirrored(g) // STRIDE
            else:
                here = 1 + g * CHUNKS + first - LOCAL
                there = 1 + mirrored(g) * CHUNKS + first
            for j in pieces:
                stage[here + j - first] = tile(g, j)
            remote(
                stage.at[pl.ds(here, number)],
                place.at[pl.ds(there, number)],
                xsend.at[phase],
                xrecv.at[phase],
                served(g),
            ).start()
        for j in pieces:
            place[0 if last else 1 + j] = tile(0, j)

    def gather(phase, hooks):
        zcopy(phase, 1).start()
        zcopy(phase, 2).start()
        hooks[0]()
        if phase:
            select(phase, 0, 1)
        for j in (1, 2):
            zcopy(phase, j).wait_recv()
            zcopy(phase, j + 2).start()
        hooks[1]()
        if not phase:
            select(phase, 0, 1)
        select(phase, 1, 2)
        for j in (3, 4):
            zcopy(phase, j).wait_recv()
            zcopy(phase, j + 2).start()
        hooks[2]()
        select(phase, 3, 2)
        zcopy(phase, 5).wait_recv()
        zcopy(phase, 6).wait_recv()
        select(phase, CHUNKS, 1)
        wait_all(phase).wait_recv()

    def wait_all(phase):
        return remote(
            stages[phase], places[phase].at[pl.ds(LOCAL, SLOTS - LOCAL)], xsend.at[phase], xrecv.at[phase], at(dx=1)
        )

    HALF_ROWS = SHARE * TILE // 2

    def ocopy(side, hop, half):
        owner = y if hop == 0 else lax.rem(y + (NY - 1 if side == 0 else 1), NY)
        part = omega_all.at[pl.ds(pl.multiple_of(owner * (2 * HALF_ROWS) + half * HALF_ROWS, HALF_ROWS), HALF_ROWS)]
        index = side * 3 + (2 if hop else half)
        return remote(part, part, osend.at[index], orecv.at[index], at(dy=1 if side == 0 else NY - 1))


    def start_hook():
        for g in range(1, GROUPS):
            remote(want_v.at[0], want_v.at[mirrored(g)], wsend, wrecv, served(g)).start()
        load_omega.wait()

        def cast(e, carry):
            low = omega_ref[e].astype(BF)
            omega_all[pl.ds(pl.multiple_of((y * SHARE + e) * TILE, TILE), TILE)] = low.T
            return carry

        lax.fori_loop(0, SHARE, cast, 0)
        for half in (0, 1):
            ocopy(0, 0, half).start()
            ocopy(1, 0, 1 - half).start()

    def table_hook():
        remote(want_v.at[pl.ds(1, GROUPS - 1)], want_v.at[pl.ds(1, GROUPS - 1)], wsend, wrecv, at(dx=1)).wait_recv()
        one = pltpu.make_async_copy(want_v, want_s, lsem.at[0])
        two = pltpu.make_async_copy(slot_v, slot_s, lsem.at[1])
        one.start()
        two.start()
        one.wait()
        two.wait()

    def forward_hook():
        ocopy(0, 0, 0).wait_recv()
        ocopy(0, 1, 0).start()
        ocopy(1, 0, 1).wait_recv()
        ocopy(1, 1, 1).start()

    gather(0, (start_hook, table_hook, forward_hook))

    own, place = zbufs[0][0], places[0]

    def put(k, tile):
        picked[k] = tile
        row = jnp.where(k < count, row_s[0, k], TR)
        for r in range(TR):
            lhs[r * NS:(r + 1) * NS, pl.ds(pl.multiple_of(k * TILE, TILE), TILE)] = jnp.where(
                row == r, tile, jnp.zeros_like(tile)
            )

    def put_own(k, carry):
        put(k, own[k])
        return carry

    def put_other(k, carry):
        put(k, place[slot_s[0, k]])
        return carry

    lax.fori_loop(0, TR, put_own, 0)
    lax.fori_loop(TR, KMAX, put_other, 0)

    def ycopy(kind, d):
        to = lax.rem(y + d, NY)
        here = pl.ds(pl.multiple_of(y * NS, NS), NS)
        there = pl.ds(pl.multiple_of(NSAMP + y * NS, NS), NS)
        mine = pl.ds(to * SHARE, SHARE)
        src, dst = (
            (picked.at[mine], rhs.at[:, here]),
            (zbufs[0][0], rows.at[:, there]),
            (zbufs[1][0], rows.at[:, here]),
            (picked_image.at[mine], rhs.at[:, there]),
        )[kind]
        return remote(src, dst, ysend.at[kind, d - 1], yrecv.at[kind, d - 1], at(dy=d))

    for side in (0, 1):
        ocopy(side, 0, 1 - side).wait_recv()
        ocopy(side, 1, side).wait_recv()

    CHUNK = 8 * TILE

    def multiply(i, total):
        part = pl.ds(pl.multiple_of(i * CHUNK, CHUNK), CHUNK)
        return total + jnp.dot(lhs[:, part], omega_all[part], preferred_element_type=jnp.float32)

    total = lax.fori_loop(0, KMAX * TILE // CHUNK, multiply, jnp.zeros((TR * NS, TILE), jnp.float32))
    image = total.astype(BF)
    for r in range(TR):
        zbufs[1][0][r] = image[r * NS:(r + 1) * NS]

    def y_hook():
        for kind in (0, 1, 2):
            for d in (1, 3, 2):
                ycopy(kind, d).start()

    gather(1, (y_hook, lambda: None, lambda: None))

    place = places[1]

    def image_own(k, carry):
        picked_image[k] = zbufs[1][0][k]
        return carry

    def image_other(k, carry):
        picked_image[k] = place[slot_s[0, k]]
        return carry

    lax.fori_loop(0, TR, image_own, 0)
    lax.fori_loop(TR, KMAX, image_other, 0)
    for d in (2, 1, 3):
        ycopy(3, d).start()

    here = pl.ds(pl.multiple_of(y * NS, NS), NS)
    there = pl.ds(pl.multiple_of(NSAMP + y * NS, NS), NS)
    for r in range(TR):
        rows[r, here] = zbufs[1][0][r]
        rows[r, there] = zbufs[0][0][r]

    def keep(e, carry):
        rhs[e, here] = picked[y * SHARE + e]
        rhs[e, there] = picked_image[y * SHARE + e]
        return carry

    lax.fori_loop(0, SHARE, keep, 0)
    for kind in (1, 2):
        for d in range(1, NY):
            ycopy(kind, d).wait_recv()
    for r in range(TR):
        rows_t[r] = rows[r].T
    for kind in (0, 3):
        for d in range(1, NY):
            ycopy(kind, d).wait_recv()

    eye = lax.broadcasted_iota(jnp.int32, (TILE, TILE), 0) == lax.broadcasted_iota(
        jnp.int32, (TILE, TILE), 1
    )

    def update(e, carry):
        k = y * SHARE + e
        gradient = jnp.dot(rows_t[row_s[0, k]], rhs[e], preferred_element_type=jnp.float32) * (0.5 / NSAMP)
        omega = omega_ref[e]
        on_diag = eye & (k < TR)
        gradient = gradient - jnp.where(on_diag, 1.0 / jnp.where(on_diag, omega, 1.0), 0.0)
        stepped = omega - gradient
        shrunk = stepped - jnp.minimum(jnp.maximum(stepped, -penalty), penalty)
        proximal = jnp.where(on_diag, stepped, shrunk)
        held = jnp.where(active_s[0, k] > 0, proximal, omega)
        out_ref[e] = jnp.where(k < count, held, 0.0)
        return carry

    lax.fori_loop(0, SHARE, update, 0)

    for phase in (0, 1):
        for j in range(1, 7):
            zcopy(phase, j).wait_send()
        wait_all(phase).wait_send()
    remote(want_v.at[pl.ds(1, GROUPS - 1)], want_v.at[pl.ds(1, GROUPS - 1)], wsend, wrecv, at(dx=1)).wait_send()
    for side in (0, 1):
        for half in (0, 1):
            ocopy(side, 0, half).wait_send()
        ocopy(side, 1, side).wait_send()
    for kind in range(4):
        for d in range(1, NY):
            ycopy(kind, d).wait_send()


def local(data, omega, tile_row, tile_col, tile_count, tile_active):
    vmem = pl.BlockSpec(memory_space=pltpu.VMEM)
    hbm = pl.BlockSpec(memory_space=pltpu.HBM)
    smem = pl.BlockSpec(memory_space=pltpu.SMEM)
    block = pltpu.VMEM((TR, NS, TILE), BF)
    scratch = [block] * (2 * (CHUNKS + 1))
    scratch += [pltpu.VMEM((SLOTS - LOCAL, NS, TILE), BF)] * 2
    scratch += [pltpu.VMEM((SLOTS, NS, TILE), BF)] * 2
    scratch += [pltpu.VMEM(data.shape, data.dtype), pltpu.VMEM(omega.shape, omega.dtype)]
    scratch += [
        pltpu.VMEM((KMAX * TILE, TILE), BF),
        pltpu.VMEM((TR * NS, KMAX * TILE), BF),
        pltpu.VMEM((KMAX, NS, TILE), BF),
        pltpu.VMEM((KMAX, NS, TILE), BF),
        pltpu.VMEM((SHARE, 2 * NSAMP, TILE), BF),
        pltpu.VMEM((TR, 2 * NSAMP, TILE), BF),
        pltpu.VMEM((TR, TILE, 2 * NSAMP), BF),
        pltpu.VMEM((GROUPS, 1, TILE), jnp.int32),
        pltpu.SMEM((GROUPS, 1, TILE), jnp.int32),
        pltpu.VMEM((1, KMAX), jnp.int32),
        pltpu.SMEM((1, KMAX), jnp.int32),
    ]
    dma = pltpu.SemaphoreType.DMA
    scratch += [dma((2, 6)), dma((2, 6)), dma((2,)), dma((2,))]
    scratch += [dma, dma, dma((4,))]
    scratch += [dma((6,)), dma((6,)), dma((4, NY - 1)), dma((4, NY - 1))]
    return pl.pallas_call(
        kernel,
        out_shape=jax.ShapeDtypeStruct(omega.shape, omega.dtype),
        in_specs=[hbm, hbm, vmem, smem, smem, smem, smem],
        out_specs=vmem,
        scratch_shapes=scratch,
        compiler_params=pltpu.CompilerParams(
            collective_id=0, has_side_effects=True, vmem_limit_bytes=60 * 2**20
        ),
    )(data, omega, tile_col, tile_row, tile_col, tile_count, tile_active)


def solution(mesh):
    placed = (
        P("samp", "var"),
        P(("var", "samp"), None, None),
        P("var", None),
        P("var", None),
        P("var"),
        P("var", None),
    )
    return jax.shard_map(
        local, mesh=mesh, in_specs=placed, out_specs=P(("var", "samp"), None, None), check_vma=False
    )
```

```python
import jax
import jax.numpy as jnp
from jax import lax
from jax.experimental import pallas as pl
from jax.experimental.pallas import tpu as pltpu
from jax.sharding import PartitionSpec as P

penalty = 0.05

NX, NZ, NC, NY = 4, 16, 2, 4
STRIDE = 3
CHUNKS = 5
PLANE = NX * NC
GROUPS = PLANE * STRIDE
LOCAL = CHUNKS
SLOTS = GROUPS * CHUNKS + PLANE
TILE = 128
TR = 8
KMAX = 64
NS = 32
SHARE = KMAX // NY
NSAMP = NS * NY
MESH = pl.DeviceIdType.MESH
BF = jnp.bfloat16


def split(g):
    if g >= GROUPS:
        dx, dc = (g - GROUPS) // NC, g % NC
        return dx, NZ - 2 if dc else 2, dc
    return g // (NC * STRIDE), (0, 1, NZ - 1)[g % STRIDE], (g // STRIDE) % NC


def mirrored(g):
    if g >= GROUPS:
        dx, dc = (g - GROUPS) // NC, g % NC
        return GROUPS + ((NX - dx) % NX) * NC + dc
    dx, dc, i = g // (NC * STRIDE), (g // STRIDE) % NC, g % STRIDE
    return (((NX - dx) % NX) * NC + dc) * STRIDE + (STRIDE - i) % STRIDE


AROUND = (0, 1, NZ - 1, 2, NZ - 2)


def kernel(
    data_hbm, omega_hbm, cols_ref, row_s, col_s, count_s, active_s, out_ref,
    *scratch,
):
    scratch = list(scratch)

    def take(n):
        got = scratch[:n]
        del scratch[:n]
        return got

    zbufs = [take(CHUNKS), take(CHUNKS)]
    stages = take(2)
    places = take(2)
    data_ref, omega_ref = take(2)
    omega_all, lhs, picked, picked_image, rhs, rhs_image, started, rows, rows_t = take(9)
    want_v, want_s, slot_v, slot_s = take(4)
    zsend, zrecv, xsend, xrecv = take(4)
    wsend, wrecv, lsem = take(3)
    osend, orecv, ysend, yrecv = take(4)

    load_data = pltpu.make_async_copy(data_hbm, data_ref, lsem.at[2])
    load_omega = pltpu.make_async_copy(omega_hbm, omega_ref, lsem.at[3])
    load_data.start()
    load_omega.start()

    var = lax.axis_index("var")
    y = lax.axis_index("samp")
    x = var // (NZ * NC)
    z = lax.rem(var // NC, NZ)
    c = lax.rem(var, NC)

    xs = [x] + [lax.rem(x + d, NX) for d in range(1, NX)]
    zs = [z] + [lax.rem(z + d, NZ) for d in range(1, NZ)]
    cs = [c, 1 - c]
    ys = [y] + [lax.rem(y + d, NY) for d in range(1, NY)]

    def at(dx=0, dz=0, dc=0, dy=0):
        return ((xs[dx] * NZ + zs[dz % NZ]) * NC + cs[dc], ys[dy])

    def served(g):
        dx, dz, dc = split(g)
        return at(dx=dx, dz=dz, dc=dc)

    def remote(src, dst, send, recv, to):
        return pltpu.make_async_remote_copy(
            src_ref=src, dst_ref=dst, send_sem=send, recv_sem=recv, device_id=to, device_id_type=MESH
        )

    barrier = pltpu.get_barrier_semaphore()
    partners = [at(dx=p // NC, dc=p % NC) for p in range(1, PLANE)]
    partners += [at(dz=dz) for dz in (1, 2, 3, NZ - 3, NZ - 2, NZ - 1)]
    partners += [at(dy=d) for d in range(1, NY)]
    for to in partners:
        pl.semaphore_signal(barrier, inc=1, device_id=to, device_id_type=MESH)

    count = count_s[0]

    lane = lax.broadcasted_iota(jnp.int32, (1, TILE), 1)

    def want(k, held):
        col = col_s[0, k]
        owner = jnp.where(k < count, col // TR, -1)
        return jnp.where(lane == owner, lax.rem(col, TR), held)

    want_v[0] = lax.fori_loop(TR, KMAX, want, jnp.zeros((1, TILE), jnp.int32), unroll=8)

    cols = cols_ref[...]
    owner = cols // TR
    dx = lax.rem(owner // (NZ * NC) - x + NX, NX)
    dz = lax.rem(lax.rem(owner // NC, NZ) - z + NZ, NZ)
    dc = lax.rem(lax.rem(owner, NC) + c, NC)
    opposite = dz == NZ // 2
    step = lax.rem(dz + NZ // 2 - 1, NZ)
    side = lax.rem(step, STRIDE)
    far = step // STRIDE
    side = jnp.where(side == 0, 2, side - 1)
    far = jnp.where(far == 2, 0, jnp.where(far == 3, 1, jnp.where(far == 1, 2, jnp.where(far == 4, 3, 4))))
    plane = dx * NC + dc
    slot_v[...] = jnp.where(
        opposite,
        GROUPS * CHUNKS + plane,
        (plane * STRIDE + side) * CHUNKS + far,
    )

    load_data.wait()
    for t in range(TR):
        zbufs[0][0][t] = data_ref[:, t * TILE:(t + 1) * TILE]

    pl.semaphore_wait(barrier, len(partners))

    PLACES = (0, STRIDE, NZ - STRIDE, 2 * STRIDE, NZ - 2 * STRIDE)

    def zcopy(phase, j):
        bufs = zbufs[phase]
        return remote(
            bufs[max(j - 2, 0)],
            bufs[j],
            zsend.at[phase, j - 1],
            zrecv.at[phase, j - 1],
            at(dz=NZ - STRIDE if j % 2 else STRIDE),
        )

    def select(phase, first, number):
        bufs, stage, place = zbufs[phase], stages[phase], places[phase]

        def tile(g, j):
            dx, dz, dc = split(g)
            table = AROUND.index(dz) * PLANE + dx * NC + dc
            return bufs[j][want_s[table, 0, at(dz=PLACES[j])[0]]]

        def send(g, here, there, pieces):
            for n, j in enumerate(pieces):
                stage[here + n] = tile(g, j)
            remote(
                stage.at[pl.ds(here, len(pieces))],
                place.at[pl.ds(there, len(pieces))],
                xsend.at[phase],
                xrecv.at[phase],
                served(g),
            ).start()

        pieces = range(first, first + number)
        if first == 3:
            for g in range(GROUPS, GROUPS + PLANE):
                base = GROUPS * CHUNKS - GROUPS
                send(g, base + g - LOCAL, base + mirrored(g), (3,) if g % NC else (4,))
        for g in range(1, GROUPS):
            send(g, g * CHUNKS + first - LOCAL, mirrored(g) * CHUNKS + first, pieces)
        for j in pieces:
            place[j] = tile(0, j)

    def gather(phase, hooks):
        zcopy(phase, 1).start()
        zcopy(phase, 2).start()
        hooks[0]()
        if phase and True:
            select(phase, 0, 1)
        for j in (1, 2):
            zcopy(phase, j).wait_recv()
            zcopy(phase, j + 2).start()
        hooks[1]()
        if not (phase and True):
            select(phase, 0, 1)
        select(phase, 1, 2)
        hooks[2]()
        for j in (3, 4):
            zcopy(phase, j).wait_recv()
        select(phase, 3, 2)
        hooks[3]()
        wait_all(phase).wait_recv()

    def wait_all(phase):
        return remote(
            stages[phase], places[phase].at[pl.ds(LOCAL, SLOTS - LOCAL)], xsend.at[phase], xrecv.at[phase], at(dx=1)
        )

    HALF_ROWS = SHARE * TILE // 2

    def ocopy(side, hop, half):
        owner = y if hop == 0 else lax.rem(y + (NY - 1 if side == 0 else 1), NY)
        part = omega_all.at[pl.ds(pl.multiple_of(owner * (2 * HALF_ROWS) + half * HALF_ROWS, HALF_ROWS), HALF_ROWS)]
        index = side * 3 + (2 if hop else half)
        return remote(part, part, osend.at[index], orecv.at[index], at(dy=1 if side == 0 else NY - 1))


    def wcopy(p):
        dx, dc = p // NC, p % NC
        there = ((NX - dx) % NX) * NC + dc
        return remote(want_v.at[0], want_v.at[there], wsend.at[0], wrecv.at[0], at(dx=dx, dc=dc))

    def wplane():
        part = want_v.at[pl.ds(1, PLANE - 1)]
        return remote(part, part, wsend.at[0], wrecv.at[0], at(dx=1))

    def wforward(i):
        there = want_v.at[pl.ds(i * PLANE, PLANE)]
        return remote(want_v.at[pl.ds(0, PLANE)], there, wsend.at[i], wrecv.at[i], at(dz=NZ - AROUND[i]))

    def start_hook():
        for p in range(1, PLANE):
            wcopy(p).start()
        load_omega.wait()

        wplane().wait_recv()
        for i in range(1, len(AROUND)):
            wforward(i).start()

        def cast(e, carry):
            low = omega_ref[e].astype(BF)
            omega_all[pl.ds(pl.multiple_of((y * SHARE + e) * TILE, TILE), TILE)] = low.T
            return carry

        lax.fori_loop(0, SHARE, cast, 0, unroll=4)
        for half in (0, 1):
            ocopy(0, 0, half).start()
            ocopy(1, 0, 1 - half).start()

    def table_hook():
        for i in range(1, len(AROUND)):
            wforward(i).wait_recv()
        one = pltpu.make_async_copy(want_v, want_s, lsem.at[0])
        two = pltpu.make_async_copy(slot_v, slot_s, lsem.at[1])
        one.start()
        two.start()
        one.wait()
        two.wait()

    def forward_hook():
        ocopy(0, 0, 0).wait_recv()
        ocopy(0, 1, 0).start()
        ocopy(1, 0, 1).wait_recv()
        ocopy(1, 1, 1).start()

    gather(0, (start_hook, table_hook, forward_hook, lambda: None))

    own, place = zbufs[0][0], places[0]

    def put(k, tile):
        picked[k] = tile
        row = jnp.where(k < count, row_s[0, k], TR)
        for r in range(TR):
            lhs[r * NS:(r + 1) * NS, pl.ds(pl.multiple_of(k * TILE, TILE), TILE)] = jnp.where(
                row == r, tile, jnp.zeros_like(tile)
            )

    def put_own(k, carry):
        put(k, own[k])
        return carry

    def put_other(k, carry):
        put(k, place[slot_s[0, k]])
        return carry

    lax.fori_loop(0, TR, put_own, 0, unroll=4)
    lax.fori_loop(TR, KMAX, put_other, 0, unroll=4)

    def ycopy(kind, d):
        to = lax.rem(y + d, NY)
        here = pl.ds(pl.multiple_of(y * NS, NS), NS)
        there = pl.ds(pl.multiple_of(NSAMP + y * NS, NS), NS)
        mine = pl.ds(to * SHARE, SHARE)
        src, dst = (
            (picked.at[mine], rhs.at[:, here]),
            (zbufs[0][0], rows.at[:, there]),
            (zbufs[1][0], rows.at[:, here]),
            (picked_image.at[mine], rhs_image.at[:, here]),
        )[kind]
        return remote(src, dst, ysend.at[kind, d - 1], yrecv.at[kind, d - 1], at(dy=d))

    for side in (0, 1):
        ocopy(side, 0, 1 - side).wait_recv()
        ocopy(side, 1, side).wait_recv()

    CHUNK = 64 * TILE

    def multiply(i, total):
        part = pl.ds(pl.multiple_of(i * CHUNK, CHUNK), CHUNK)
        return total + jnp.dot(lhs[:, part], omega_all[part], preferred_element_type=jnp.float32)

    total = lax.fori_loop(0, KMAX * TILE // CHUNK, multiply, jnp.zeros((TR * NS, TILE), jnp.float32))
    image = total.astype(BF)
    for r in range(TR):
        zbufs[1][0][r] = image[r * NS:(r + 1) * NS]

    def y_hook():
        for kind in (0, 1, 2):
            for d in (1, 3, 2):
                ycopy(kind, d).start()

    eye = lax.broadcasted_iota(jnp.int32, (TILE, TILE), 0) == lax.broadcasted_iota(
        jnp.int32, (TILE, TILE), 1
    )

    def early_hook():
        here = pl.ds(pl.multiple_of(y * NS, NS), NS)
        there = pl.ds(pl.multiple_of(NSAMP + y * NS, NS), NS)
        for r in range(TR):
            rows[r, here] = zbufs[1][0][r]
            rows[r, there] = zbufs[0][0][r]

        def keep(e, carry):
            rhs[e, here] = picked[y * SHARE + e]
            return carry

        lax.fori_loop(0, SHARE, keep, 0, unroll=8)
        for kind in (0, 1, 2):
            for d in range(1, NY):
                ycopy(kind, d).wait_recv()
        for r in range(TR):
            rows_t[r] = rows[r].T

        def start(e, carry):
            k = y * SHARE + e
            gradient = jnp.dot(rows_t[row_s[0, k], :, :NSAMP], rhs[e], preferred_element_type=jnp.float32)
            omega = omega_ref[e]
            on_diag = eye & (k < TR)
            inverse = jnp.where(on_diag, 1.0 / jnp.where(on_diag, omega, 1.0), 0.0)
            started[e] = omega - (gradient * (0.5 / NSAMP) - inverse)
            return carry

        lax.fori_loop(0, SHARE, start, 0, unroll=4)

    gather(1, (y_hook, lambda: None, lambda: None, early_hook))

    place = places[1]

    def image_own(k, carry):
        picked_image[k] = zbufs[1][0][k]
        return carry

    def image_other(k, carry):
        picked_image[k] = place[slot_s[0, k]]
        return carry

    lax.fori_loop(0, TR, image_own, 0, unroll=8)
    lax.fori_loop(TR, KMAX, image_other, 0, unroll=8)
    for d in (2, 1, 3):
        ycopy(3, d).start()

    def last(e, carry):
        rhs_image[e, pl.ds(pl.multiple_of(y * NS, NS), NS)] = picked_image[y * SHARE + e]
        return carry

    lax.fori_loop(0, SHARE, last, 0, unroll=8)
    for d in range(1, NY):
        ycopy(3, d).wait_recv()

    def update(e, carry):
        k = y * SHARE + e
        gradient = jnp.dot(rows_t[row_s[0, k], :, NSAMP:], rhs_image[e], preferred_element_type=jnp.float32)
        stepped = started[e] - gradient * (0.5 / NSAMP)
        shrunk = stepped - jnp.minimum(jnp.maximum(stepped, -penalty), penalty)
        proximal = jnp.where(eye & (k < TR), stepped, shrunk)
        held = jnp.where(active_s[0, k] > 0, proximal, omega_ref[e])
        out_ref[e] = jnp.where(k < count, held, 0.0)
        return carry

    lax.fori_loop(0, SHARE, update, 0, unroll=4)

    for phase in (0, 1):
        for j in range(1, CHUNKS):
            zcopy(phase, j).wait_send()
        wait_all(phase).wait_send()
    wplane().wait_send()
    for i in range(1, len(AROUND)):
        wforward(i).wait_send()
    for side in (0, 1):
        for half in (0, 1):
            ocopy(side, 0, half).wait_send()
        ocopy(side, 1, side).wait_send()
    for kind in range(4):
        for d in range(1, NY):
            ycopy(kind, d).wait_send()


def local(data, omega, tile_row, tile_col, tile_count, tile_active):
    vmem = pl.BlockSpec(memory_space=pltpu.VMEM)
    hbm = pl.BlockSpec(memory_space=pltpu.HBM)
    smem = pl.BlockSpec(memory_space=pltpu.SMEM)
    block = pltpu.VMEM((TR, NS, TILE), BF)
    scratch = [block] * (2 * CHUNKS)
    scratch += [pltpu.VMEM((SLOTS - LOCAL, NS, TILE), BF)] * 2
    scratch += [pltpu.VMEM((SLOTS, NS, TILE), BF)] * 2
    scratch += [pltpu.VMEM(data.shape, data.dtype), pltpu.VMEM(omega.shape, omega.dtype)]
    scratch += [
        pltpu.VMEM((KMAX * TILE, TILE), BF),
        pltpu.VMEM((TR * NS, KMAX * TILE), BF),
        pltpu.VMEM((KMAX, NS, TILE), BF),
        pltpu.VMEM((KMAX, NS, TILE), BF),
        pltpu.VMEM((SHARE, NSAMP, TILE), BF),
        pltpu.VMEM((SHARE, NSAMP, TILE), BF),
        pltpu.VMEM((SHARE, TILE, TILE), jnp.float32),
        pltpu.VMEM((TR, 2 * NSAMP, TILE), BF),
        pltpu.VMEM((TR, TILE, 2 * NSAMP), BF),
        pltpu.VMEM((len(AROUND) * PLANE, 1, TILE), jnp.int32),
        pltpu.SMEM((len(AROUND) * PLANE, 1, TILE), jnp.int32),
        pltpu.VMEM((1, KMAX), jnp.int32),
        pltpu.SMEM((1, KMAX), jnp.int32),
    ]
    dma = pltpu.SemaphoreType.DMA
    scratch += [dma((2, CHUNKS - 1)), dma((2, CHUNKS - 1)), dma((2,)), dma((2,))]
    scratch += [dma((len(AROUND),)), dma((len(AROUND),)), dma((4,))]
    scratch += [dma((6,)), dma((6,)), dma((4, NY - 1)), dma((4, NY - 1))]
    return pl.pallas_call(
        kernel,
        out_shape=jax.ShapeDtypeStruct(omega.shape, omega.dtype),
        in_specs=[hbm, hbm, vmem, smem, smem, smem, smem],
        out_specs=vmem,
        scratch_shapes=scratch,
        compiler_params=pltpu.CompilerParams(
            collective_id=0, has_side_effects=True, vmem_limit_bytes=32 * 2**20
        ),
    )(data, omega, tile_col, tile_row, tile_col, tile_count, tile_active)


def solution(mesh):
    placed = (
        P("samp", "var"),
        P(("var", "samp"), None, None),
        P("var", None),
        P("var", None),
        P("var"),
        P("var", None),
    )
    return jax.shard_map(
        local, mesh=mesh, in_specs=placed, out_specs=P(("var", "samp"), None, None), check_vma=False
    )
```

```python
import jax
import jax.numpy as jnp
from jax import lax
from jax.experimental import pallas as pl
from jax.experimental.pallas import tpu as pltpu
from jax.sharding import PartitionSpec as P

penalty = 0.05

NX, NZ, NC, NY = 4, 16, 2, 4
STRIDE = 3
CHUNKS = 5
PLANE = NX * NC
GROUPS = PLANE * STRIDE
LOCAL = CHUNKS
SLOTS = GROUPS * CHUNKS + PLANE
TILE = 128
TR = 8
KMAX = 64
NS = 32
SHARE = KMAX // NY
NSAMP = NS * NY
MESH = pl.DeviceIdType.MESH
BF = jnp.bfloat16


def split(g):
    if g >= GROUPS:
        dx, dc = (g - GROUPS) // NC, g % NC
        return dx, NZ - 2 if dc else 2, dc
    return g // (NC * STRIDE), (0, 1, NZ - 1)[g % STRIDE], (g // STRIDE) % NC


def mirrored(g):
    if g >= GROUPS:
        dx, dc = (g - GROUPS) // NC, g % NC
        return GROUPS + ((NX - dx) % NX) * NC + dc
    dx, dc, i = g // (NC * STRIDE), (g // STRIDE) % NC, g % STRIDE
    return (((NX - dx) % NX) * NC + dc) * STRIDE + (STRIDE - i) % STRIDE


def links(g):
    dx, dz, dc = split(g)
    return 2 * min(dx, NX - dx) + min(dz, NZ - dz)


FAR_FIRST = sorted(range(1, GROUPS), key=lambda g: -links(g))

AROUND = (0, 1, NZ - 1, 2, NZ - 2)


def kernel(
    data_hbm, omega_hbm, cols_ref, row_s, col_s, count_s, active_s, out_ref,
    *scratch,
):
    scratch = list(scratch)

    def take(n):
        got = scratch[:n]
        del scratch[:n]
        return got

    zbufs = [take(CHUNKS), take(CHUNKS)]
    stages = take(2)
    places = take(2)
    data_ref, omega_ref = take(2)
    omega_all, lhs, picked, picked_image, rhs, rhs_image, started, rows, rows_t = take(9)
    want_v, want_s, slot_v, slot_s = take(4)
    zsend, zrecv, xsend, xrecv = take(4)
    wsend, wrecv, lsem = take(3)
    osend, orecv, ysend, yrecv, lsend, lrecv = take(6)

    load_data = pltpu.make_async_copy(data_hbm, data_ref, lsem.at[2])
    load_omega = pltpu.make_async_copy(omega_hbm, omega_ref, lsem.at[3])
    load_data.start()
    load_omega.start()

    var = lax.axis_index("var")
    y = lax.axis_index("samp")
    x = var // (NZ * NC)
    z = lax.rem(var // NC, NZ)
    c = lax.rem(var, NC)

    xs = [x] + [lax.rem(x + d, NX) for d in range(1, NX)]
    zs = [z] + [lax.rem(z + d, NZ) for d in range(1, NZ)]
    cs = [c, 1 - c]
    ys = [y] + [lax.rem(y + d, NY) for d in range(1, NY)]

    def at(dx=0, dz=0, dc=0, dy=0):
        return ((xs[dx] * NZ + zs[dz % NZ]) * NC + cs[dc], ys[dy])

    def served(g):
        dx, dz, dc = split(g)
        return at(dx=dx, dz=dz, dc=dc)

    def remote(src, dst, send, recv, to):
        return pltpu.make_async_remote_copy(
            src_ref=src, dst_ref=dst, send_sem=send, recv_sem=recv, device_id=to, device_id_type=MESH
        )

    barrier = pltpu.get_barrier_semaphore()
    partners = [at(dx=p // NC, dc=p % NC) for p in range(1, PLANE)]
    partners += [at(dz=dz) for dz in (1, 2, 3, NZ - 3, NZ - 2, NZ - 1)]
    partners += [at(dy=d) for d in range(1, NY)]
    for to in partners:
        pl.semaphore_signal(barrier, inc=1, device_id=to, device_id_type=MESH)

    count = count_s[0]

    lane = lax.broadcasted_iota(jnp.int32, (1, TILE), 1)

    def want(k, held):
        col = col_s[0, k]
        owner = jnp.where(k < count, col // TR, -1)
        return jnp.where(lane == owner, lax.rem(col, TR), held)

    want_v[0] = lax.fori_loop(TR, KMAX, want, jnp.zeros((1, TILE), jnp.int32), unroll=8)

    cols = cols_ref[...]
    owner = cols // TR
    dx = lax.rem(owner // (NZ * NC) - x + NX, NX)
    dz = lax.rem(lax.rem(owner // NC, NZ) - z + NZ, NZ)
    dc = lax.rem(lax.rem(owner, NC) + c, NC)
    opposite = dz == NZ // 2
    step = lax.rem(dz + NZ // 2 - 1, NZ)
    side = lax.rem(step, STRIDE)
    far = step // STRIDE
    side = jnp.where(side == 0, 2, side - 1)
    far = jnp.where(far == 2, 0, jnp.where(far == 3, 1, jnp.where(far == 1, 2, jnp.where(far == 4, 3, 4))))
    plane = dx * NC + dc
    entry = lax.broadcasted_iota(jnp.int32, cols.shape, 1)
    slot_v[...] = jnp.where(entry < TR, SLOTS + entry, jnp.where(
        opposite,
        GROUPS * CHUNKS + plane,
        (plane * STRIDE + side) * CHUNKS + far,
    ))

    load_data.wait()
    for t in range(TR):
        zbufs[0][0][t] = data_ref[:, t * TILE:(t + 1) * TILE]

    pl.semaphore_wait(barrier, len(partners))

    PLACES = (0, STRIDE, NZ - STRIDE, 2 * STRIDE, NZ - 2 * STRIDE)

    def zcopy(phase, j):
        bufs = zbufs[phase]
        return remote(
            bufs[max(j - 2, 0)],
            bufs[j],
            zsend.at[phase, j - 1],
            zrecv.at[phase, j - 1],
            at(dz=NZ - STRIDE if j % 2 else STRIDE),
        )

    def select(phase, first, number):
        bufs, stage, place = zbufs[phase], stages[phase], places[phase]

        def tile(g, j):
            dx, dz, dc = split(g)
            table = AROUND.index(dz) * PLANE + dx * NC + dc
            return bufs[j][want_s[table, 0, at(dz=PLACES[j])[0]]]

        def send(g, here, there, pieces):
            for n, j in enumerate(pieces):
                stage[here + n] = tile(g, j)
            remote(
                stage.at[pl.ds(here, len(pieces))],
                place.at[pl.ds(there, len(pieces))],
                xsend.at[phase],
                xrecv.at[phase],
                served(g),
            ).start()

        pieces = range(first, first + number)
        if first == 3:
            for g in range(GROUPS, GROUPS + PLANE):
                base = GROUPS * CHUNKS - GROUPS
                send(g, base + g - LOCAL, base + mirrored(g), (3,) if g % NC else (4,))
        for g in FAR_FIRST:
            send(g, g * CHUNKS + first - LOCAL, mirrored(g) * CHUNKS + first, pieces)
        for j in pieces:
            place[j] = tile(0, j)
        if first == 3:
            for t in range(TR):
                place[SLOTS + t] = bufs[0][t]

    def gather(phase, hooks):
        zcopy(phase, 1).start()
        zcopy(phase, 2).start()
        hooks[0]()
        if phase and True:
            select(phase, 0, 1)
        for j in (1, 2):
            zcopy(phase, j).wait_recv()
            zcopy(phase, j + 2).start()
        hooks[1]()
        if not (phase and True):
            select(phase, 0, 1)
        select(phase, 1, 2)
        hooks[2]()
        for j in (3, 4):
            zcopy(phase, j).wait_recv()
        select(phase, 3, 2)
        hooks[3]()
        wait_all(phase).wait_recv()

    def wait_all(phase):
        return remote(
            stages[phase], places[phase].at[pl.ds(LOCAL, SLOTS - LOCAL)], xsend.at[phase], xrecv.at[phase], at(dx=1)
        )

    HALF_ROWS = SHARE * TILE // 2

    def ocopy(side, hop, half):
        owner = y if hop == 0 else lax.rem(y + (NY - 1 if side == 0 else 1), NY)
        part = omega_all.at[pl.ds(pl.multiple_of(owner * (2 * HALF_ROWS) + half * HALF_ROWS, HALF_ROWS), HALF_ROWS)]
        index = side * 3 + (2 if hop else half)
        return remote(part, part, osend.at[index], orecv.at[index], at(dy=1 if side == 0 else NY - 1))


    def wcopy(p):
        dx, dc = p // NC, p % NC
        there = ((NX - dx) % NX) * NC + dc
        return remote(want_v.at[0], want_v.at[there], wsend.at[0], wrecv.at[0], at(dx=dx, dc=dc))

    def wplane():
        part = want_v.at[pl.ds(1, PLANE - 1)]
        return remote(part, part, wsend.at[0], wrecv.at[0], at(dx=1))

    def wforward(i):
        there = want_v.at[pl.ds(i * PLANE, PLANE)]
        return remote(want_v.at[pl.ds(0, PLANE)], there, wsend.at[i], wrecv.at[i], at(dz=NZ - AROUND[i]))

    def start_hook():
        for p in range(1, PLANE):
            wcopy(p).start()
        load_omega.wait()

        wplane().wait_recv()
        for i in range(1, len(AROUND)):
            wforward(i).start()

        def cast(e, carry):
            low = omega_ref[e].astype(BF)
            omega_all[pl.ds(pl.multiple_of((y * SHARE + e) * TILE, TILE), TILE)] = low.T
            return carry

        lax.fori_loop(0, SHARE, cast, 0, unroll=4)
        for half in (0, 1):
            ocopy(0, 0, half).start()
            ocopy(1, 0, 1 - half).start()

    def table_hook():
        for i in range(1, len(AROUND)):
            wforward(i).wait_recv()
        one = pltpu.make_async_copy(want_v, want_s, lsem.at[0])
        two = pltpu.make_async_copy(slot_v, slot_s, lsem.at[1])
        one.start()
        two.start()
        one.wait()
        two.wait()

    def forward_hook():
        ocopy(0, 0, 0).wait_recv()
        ocopy(0, 1, 0).start()
        ocopy(1, 0, 1).wait_recv()
        ocopy(1, 1, 1).start()

    gather(0, (start_hook, table_hook, forward_hook, lambda: None))

    own, place = zbufs[0][0], places[0]

    def put(k, tile):
        picked[k] = tile
        row = jnp.where(k < count, row_s[0, k], TR)
        for r in range(TR):
            lhs[r * NS:(r + 1) * NS, pl.ds(pl.multiple_of(k * TILE, TILE), TILE)] = jnp.where(
                row == r, tile, jnp.zeros_like(tile)
            )

    def put_own(k, carry):
        put(k, own[k])
        return carry

    def put_other(k, carry):
        put(k, place[slot_s[0, k]])
        return carry

    lax.fori_loop(0, TR, put_own, 0, unroll=4)
    lax.fori_loop(TR, KMAX, put_other, 0, unroll=4)

    def ycopy(kind, d):
        to = lax.rem(y + d, NY)
        here = pl.ds(pl.multiple_of(y * NS, NS), NS)
        there = pl.ds(pl.multiple_of(NSAMP + y * NS, NS), NS)
        mine = pl.ds(to * SHARE, SHARE)
        src, dst = (
            (picked.at[mine], rhs.at[:, here]),
            (zbufs[0][0], rows.at[:, there]),
            (zbufs[1][0], rows.at[:, here]),
            (None, None),
        )[kind]
        return remote(src, dst, ysend.at[kind, d - 1], yrecv.at[kind, d - 1], at(dy=d))

    for side in (0, 1):
        ocopy(side, 0, 1 - side).wait_recv()
        ocopy(side, 1, side).wait_recv()

    CHUNK = 64 * TILE

    def multiply(i, total):
        part = pl.ds(pl.multiple_of(i * CHUNK, CHUNK), CHUNK)
        return total + jnp.dot(lhs[:, part], omega_all[part], preferred_element_type=jnp.float32)

    total = lax.fori_loop(0, KMAX * TILE // CHUNK, multiply, jnp.zeros((TR * NS, TILE), jnp.float32))
    image = total.astype(BF)
    for r in range(TR):
        zbufs[1][0][r] = image[r * NS:(r + 1) * NS]

    def y_hook():
        for kind in (0, 1, 2):
            for d in (1, 3, 2):
                ycopy(kind, d).start()

    eye = lax.broadcasted_iota(jnp.int32, (TILE, TILE), 0) == lax.broadcasted_iota(
        jnp.int32, (TILE, TILE), 1
    )

    def early_hook():
        here = pl.ds(pl.multiple_of(y * NS, NS), NS)
        there = pl.ds(pl.multiple_of(NSAMP + y * NS, NS), NS)
        for r in range(TR):
            rows[r, here] = zbufs[1][0][r]
            rows[r, there] = zbufs[0][0][r]

        def keep(e, carry):
            rhs[e, here] = picked[y * SHARE + e]
            return carry

        lax.fori_loop(0, SHARE, keep, 0, unroll=8)
        for kind in (0, 1, 2):
            for d in range(1, NY):
                ycopy(kind, d).wait_recv()
        for r in range(TR):
            rows_t[r] = rows[r].T

        def start(e, carry):
            k = y * SHARE + e
            gradient = jnp.dot(rows_t[row_s[0, k], :, :NSAMP], rhs[e], preferred_element_type=jnp.float32)
            omega = omega_ref[e]
            on_diag = eye & (k < TR)
            inverse = jnp.where(on_diag, 1.0 / jnp.where(on_diag, omega, 1.0), 0.0)
            started[e] = omega - (gradient * (0.5 / NSAMP) - inverse)
            return carry

        lax.fori_loop(0, SHARE, start, 0, unroll=4)

    gather(1, (lambda: None, y_hook, lambda: None, early_hook))

    place = places[1]

    PART = SHARE // 2

    def lastcopy(d, half):
        here = pl.ds(pl.multiple_of(y * NS, NS), NS)
        return remote(
            picked_image.at[pl.ds(ys[d] * SHARE + half * PART, PART)],
            rhs_image.at[pl.ds(half * PART, PART), here],
            lsend.at[half, d - 1],
            lrecv.at[half, d - 1],
            at(dy=d),
        )

    for half in (0, 1):
        for d in (2, 1, 3, 0):
            for e in range(half * PART, (half + 1) * PART):
                k = ys[d] * SHARE + e
                tile = place[slot_s[0, k]]
                if d:
                    picked_image[k] = tile
                else:
                    rhs_image[e, pl.ds(pl.multiple_of(y * NS, NS), NS)] = tile
            if d:
                lastcopy(d, half).start()

    def update(e, carry):
        k = y * SHARE + e
        gradient = jnp.dot(rows_t[row_s[0, k], :, NSAMP:], rhs_image[e], preferred_element_type=jnp.float32)
        stepped = started[e] - gradient * (0.5 / NSAMP)
        shrunk = stepped - jnp.minimum(jnp.maximum(stepped, -penalty), penalty)
        proximal = jnp.where(eye & (k < TR), stepped, shrunk)
        held = jnp.where(active_s[0, k] > 0, proximal, omega_ref[e])
        out_ref[e] = jnp.where(k < count, held, 0.0)
        return carry

    for half in (0, 1):
        for d in range(1, NY):
            lastcopy(d, half).wait_recv()
        lax.fori_loop(half * PART, (half + 1) * PART, update, 0, unroll=4)

    for phase in (0, 1):
        for j in range(1, CHUNKS):
            zcopy(phase, j).wait_send()
        wait_all(phase).wait_send()
    wplane().wait_send()
    for i in range(1, len(AROUND)):
        wforward(i).wait_send()
    for side in (0, 1):
        for half in (0, 1):
            ocopy(side, 0, half).wait_send()
        ocopy(side, 1, side).wait_send()
    for d in range(1, NY):
        for kind in range(3):
            ycopy(kind, d).wait_send()
        for half in (0, 1):
            lastcopy(d, half).wait_send()


def local(data, omega, tile_row, tile_col, tile_count, tile_active):
    vmem = pl.BlockSpec(memory_space=pltpu.VMEM)
    hbm = pl.BlockSpec(memory_space=pltpu.HBM)
    smem = pl.BlockSpec(memory_space=pltpu.SMEM)
    block = pltpu.VMEM((TR, NS, TILE), BF)
    scratch = [block] * (2 * CHUNKS)
    scratch += [pltpu.VMEM((SLOTS - LOCAL, NS, TILE), BF)] * 2
    scratch += [pltpu.VMEM((SLOTS + TR, NS, TILE), BF)] * 2
    scratch += [pltpu.VMEM(data.shape, data.dtype), pltpu.VMEM(omega.shape, omega.dtype)]
    scratch += [
        pltpu.VMEM((KMAX * TILE, TILE), BF),
        pltpu.VMEM((TR * NS, KMAX * TILE), BF),
        pltpu.VMEM((KMAX, NS, TILE), BF),
        pltpu.VMEM((KMAX, NS, TILE), BF),
        pltpu.VMEM((SHARE, NSAMP, TILE), BF),
        pltpu.VMEM((SHARE, NSAMP, TILE), BF),
        pltpu.VMEM((SHARE, TILE, TILE), jnp.float32),
        pltpu.VMEM((TR, 2 * NSAMP, TILE), BF),
        pltpu.VMEM((TR, TILE, 2 * NSAMP), BF),
        pltpu.VMEM((len(AROUND) * PLANE, 1, TILE), jnp.int32),
        pltpu.SMEM((len(AROUND) * PLANE, 1, TILE), jnp.int32),
        pltpu.VMEM((1, KMAX), jnp.int32),
        pltpu.SMEM((1, KMAX), jnp.int32),
    ]
    dma = pltpu.SemaphoreType.DMA
    scratch += [dma((2, CHUNKS - 1)), dma((2, CHUNKS - 1)), dma((2,)), dma((2,))]
    scratch += [dma((len(AROUND),)), dma((len(AROUND),)), dma((4,))]
    scratch += [dma((6,)), dma((6,)), dma((3, NY - 1)), dma((3, NY - 1)), dma((2, NY - 1)), dma((2, NY - 1))]
    return pl.pallas_call(
        kernel,
        out_shape=jax.ShapeDtypeStruct(omega.shape, omega.dtype),
        in_specs=[hbm, hbm, vmem, smem, smem, smem, smem],
        out_specs=vmem,
        scratch_shapes=scratch,
        compiler_params=pltpu.CompilerParams(
            collective_id=0, has_side_effects=True, vmem_limit_bytes=32 * 2**20
        ),
    )(data, omega, tile_col, tile_row, tile_col, tile_count, tile_active)


def solution(mesh):
    placed = (
        P("samp", "var"),
        P(("var", "samp"), None, None),
        P("var", None),
        P("var", None),
        P("var"),
        P("var", None),
    )
    return jax.shard_map(
        local, mesh=mesh, in_specs=placed, out_specs=P(("var", "samp"), None, None), check_vma=False
    )
```

```python
import jax
import jax.numpy as jnp
from jax import lax
from jax.experimental import pallas as pl
from jax.experimental.pallas import tpu as pltpu
from jax.sharding import PartitionSpec as P

penalty = 0.05

NX, NZ, NC, NY = 4, 16, 2, 4
STRIDE = 3
CHUNKS = 5
PLANE = NX * NC
GROUPS = PLANE * STRIDE
LOCAL = CHUNKS
SLOTS = GROUPS * CHUNKS + PLANE
TILE = 128
TR = 8
KMAX = 64
NS = 32
SHARE = KMAX // NY
NSAMP = NS * NY
MESH = pl.DeviceIdType.MESH
BF = jnp.bfloat16


def split(g):
    if g >= GROUPS:
        dx, dc = (g - GROUPS) // NC, g % NC
        return dx, NZ - 2 if dc else 2, dc
    return g // (NC * STRIDE), (0, 1, NZ - 1)[g % STRIDE], (g // STRIDE) % NC


def mirrored(g):
    if g >= GROUPS:
        dx, dc = (g - GROUPS) // NC, g % NC
        return GROUPS + ((NX - dx) % NX) * NC + dc
    dx, dc, i = g // (NC * STRIDE), (g // STRIDE) % NC, g % STRIDE
    return (((NX - dx) % NX) * NC + dc) * STRIDE + (STRIDE - i) % STRIDE


def links(g):
    dx, dz, dc = split(g)
    return 2 * min(dx, NX - dx) + min(dz, NZ - dz)


FAR_FIRST = sorted(range(1, GROUPS), key=lambda g: -links(g))

AROUND = (0, 1, NZ - 1, 2, NZ - 2)


def kernel(
    data_hbm, omega_hbm, cols_ref, row_s, col_s, count_s, active_s, out_hbm,
    *scratch,
):
    scratch = list(scratch)

    def take(n):
        got = scratch[:n]
        del scratch[:n]
        return got

    zbufs = [take(CHUNKS), take(CHUNKS)]
    stages = take(2)
    places = take(2)
    data_ref, omega_ref, out_ref = take(3)
    omega_all, lhs, picked, picked_image, rhs, rhs_image, started, rows, rows_t = take(9)
    want_v, want_s, slot_v, slot_s = take(4)
    zsend, zrecv, xsend, xrecv = take(4)
    wsend, wrecv, lsem = take(3)
    osend, orecv, ysend, yrecv, lsend, lrecv = take(6)

    load_data = pltpu.make_async_copy(data_hbm, data_ref, lsem.at[2])
    load_omega = pltpu.make_async_copy(omega_hbm, omega_ref, lsem.at[3])
    load_data.start()
    load_omega.start()

    var = lax.axis_index("var")
    y = lax.axis_index("samp")
    x = var // (NZ * NC)
    z = lax.rem(var // NC, NZ)
    c = lax.rem(var, NC)

    xs = [x] + [lax.rem(x + d, NX) for d in range(1, NX)]
    zs = [z] + [lax.rem(z + d, NZ) for d in range(1, NZ)]
    cs = [c, 1 - c]
    ys = [y] + [lax.rem(y + d, NY) for d in range(1, NY)]

    def at(dx=0, dz=0, dc=0, dy=0):
        return ((xs[dx] * NZ + zs[dz % NZ]) * NC + cs[dc], ys[dy])

    def served(g):
        dx, dz, dc = split(g)
        return at(dx=dx, dz=dz, dc=dc)

    def remote(src, dst, send, recv, to):
        return pltpu.make_async_remote_copy(
            src_ref=src, dst_ref=dst, send_sem=send, recv_sem=recv, device_id=to, device_id_type=MESH
        )

    barrier = pltpu.get_barrier_semaphore()
    partners = [at(dx=p // NC, dc=p % NC) for p in range(1, PLANE)]
    partners += [at(dz=dz) for dz in (1, 2, 3, NZ - 3, NZ - 2, NZ - 1)]
    partners += [at(dy=d) for d in range(1, NY)]
    for to in partners:
        pl.semaphore_signal(barrier, inc=1, device_id=to, device_id_type=MESH)

    count = count_s[0]

    lane = lax.broadcasted_iota(jnp.int32, (1, TILE), 1)

    def want(k, held):
        col = col_s[0, k]
        owner = jnp.where(k < count, col // TR, -1)
        return jnp.where(lane == owner, lax.rem(col, TR), held)

    want_v[0] = lax.fori_loop(TR, KMAX, want, jnp.zeros((1, TILE), jnp.int32), unroll=8)

    cols = cols_ref[...]
    owner = cols // TR
    dx = lax.rem(owner // (NZ * NC) - x + NX, NX)
    dz = lax.rem(lax.rem(owner // NC, NZ) - z + NZ, NZ)
    dc = lax.rem(lax.rem(owner, NC) + c, NC)
    opposite = dz == NZ // 2
    step = lax.rem(dz + NZ // 2 - 1, NZ)
    side = lax.rem(step, STRIDE)
    far = step // STRIDE
    side = jnp.where(side == 0, 2, side - 1)
    far = jnp.where(far == 2, 0, jnp.where(far == 3, 1, jnp.where(far == 1, 2, jnp.where(far == 4, 3, 4))))
    plane = dx * NC + dc
    entry = lax.broadcasted_iota(jnp.int32, cols.shape, 1)
    slot_v[...] = jnp.where(entry < TR, SLOTS + entry, jnp.where(
        opposite,
        GROUPS * CHUNKS + plane,
        (plane * STRIDE + side) * CHUNKS + far,
    ))

    load_data.wait()
    for t in range(TR):
        zbufs[0][0][t] = data_ref[:, t * TILE:(t + 1) * TILE]

    pl.semaphore_wait(barrier, len(partners))

    PLACES = (0, STRIDE, NZ - STRIDE, 2 * STRIDE, NZ - 2 * STRIDE)

    def zcopy(phase, j):
        bufs = zbufs[phase]
        return remote(
            bufs[max(j - 2, 0)],
            bufs[j],
            zsend.at[phase, j - 1],
            zrecv.at[phase, j - 1],
            at(dz=NZ - STRIDE if j % 2 else STRIDE),
        )

    def select(phase, first, number):
        bufs, stage, place = zbufs[phase], stages[phase], places[phase]

        def tile(g, j):
            dx, dz, dc = split(g)
            table = AROUND.index(dz) * PLANE + dx * NC + dc
            return bufs[j][want_s[table, 0, at(dz=PLACES[j])[0]]]

        def send(g, here, there, pieces):
            for n, j in enumerate(pieces):
                stage[here + n] = tile(g, j)
            remote(
                stage.at[pl.ds(here, len(pieces))],
                place.at[pl.ds(there, len(pieces))],
                xsend.at[phase],
                xrecv.at[phase],
                served(g),
            ).start()

        pieces = range(first, first + number)
        if first == 3:
            for g in range(GROUPS, GROUPS + PLANE):
                base = GROUPS * CHUNKS - GROUPS
                send(g, base + g - LOCAL, base + mirrored(g), (3,) if g % NC else (4,))
        for g in FAR_FIRST:
            send(g, g * CHUNKS + first - LOCAL, mirrored(g) * CHUNKS + first, pieces)
        for j in pieces:
            place[j] = tile(0, j)
        if first == 3:
            for t in range(TR):
                place[SLOTS + t] = bufs[0][t]

    def gather(phase, hooks):
        zcopy(phase, 1).start()
        zcopy(phase, 2).start()
        hooks[0]()
        if phase and True:
            select(phase, 0, 1)
        for j in (1, 2):
            zcopy(phase, j).wait_recv()
            zcopy(phase, j + 2).start()
        hooks[1]()
        if not (phase and True):
            select(phase, 0, 1)
        select(phase, 1, 2)
        hooks[2]()
        for j in (3, 4):
            zcopy(phase, j).wait_recv()
        select(phase, 3, 2)
        hooks[3]()
        wait_all(phase).wait_recv()

    def wait_all(phase):
        return remote(
            stages[phase], places[phase].at[pl.ds(LOCAL, SLOTS - LOCAL)], xsend.at[phase], xrecv.at[phase], at(dx=1)
        )

    HALF_ROWS = SHARE * TILE // 2

    def ocopy(side, hop, half):
        owner = y if hop == 0 else lax.rem(y + (NY - 1 if side == 0 else 1), NY)
        part = omega_all.at[pl.ds(pl.multiple_of(owner * (2 * HALF_ROWS) + half * HALF_ROWS, HALF_ROWS), HALF_ROWS)]
        index = side * 3 + (2 if hop else half)
        return remote(part, part, osend.at[index], orecv.at[index], at(dy=1 if side == 0 else NY - 1))


    def wcopy(p):
        dx, dc = p // NC, p % NC
        there = ((NX - dx) % NX) * NC + dc
        return remote(want_v.at[0], want_v.at[there], wsend.at[0], wrecv.at[0], at(dx=dx, dc=dc))

    def wplane():
        part = want_v.at[pl.ds(1, PLANE - 1)]
        return remote(part, part, wsend.at[0], wrecv.at[0], at(dx=1))

    def wforward(i):
        there = want_v.at[pl.ds(i * PLANE, PLANE)]
        return remote(want_v.at[pl.ds(0, PLANE)], there, wsend.at[i], wrecv.at[i], at(dz=NZ - AROUND[i]))

    def start_hook():
        for p in range(1, PLANE):
            wcopy(p).start()
        load_omega.wait()

        wplane().wait_recv()
        for i in range(1, len(AROUND)):
            wforward(i).start()

        def cast(e, carry):
            low = omega_ref[e].astype(BF)
            omega_all[pl.ds(pl.multiple_of((y * SHARE + e) * TILE, TILE), TILE)] = low.T
            return carry

        lax.fori_loop(0, SHARE, cast, 0, unroll=4)
        for half in (0, 1):
            ocopy(0, 0, half).start()
            ocopy(1, 0, 1 - half).start()

    def table_hook():
        for i in range(1, len(AROUND)):
            wforward(i).wait_recv()
        one = pltpu.make_async_copy(want_v, want_s, lsem.at[0])
        two = pltpu.make_async_copy(slot_v, slot_s, lsem.at[1])
        one.start()
        two.start()
        one.wait()
        two.wait()

    def forward_hook():
        ocopy(0, 0, 0).wait_recv()
        ocopy(0, 1, 0).start()
        ocopy(1, 0, 1).wait_recv()
        ocopy(1, 1, 1).start()

    gather(0, (start_hook, table_hook, forward_hook, lambda: None))

    own, place = zbufs[0][0], places[0]

    def put(k, tile):
        picked[k] = tile
        row = jnp.where(k < count, row_s[0, k], TR)
        for r in range(TR):
            lhs[r * NS:(r + 1) * NS, pl.ds(pl.multiple_of(k * TILE, TILE), TILE)] = jnp.where(
                row == r, tile, jnp.zeros_like(tile)
            )

    def put_own(k, carry):
        put(k, own[k])
        return carry

    def put_other(k, carry):
        put(k, place[slot_s[0, k]])
        return carry

    lax.fori_loop(0, TR, put_own, 0, unroll=4)
    lax.fori_loop(TR, KMAX, put_other, 0, unroll=4)

    def ycopy(kind, d):
        to = lax.rem(y + d, NY)
        here = pl.ds(pl.multiple_of(y * NS, NS), NS)
        there = pl.ds(pl.multiple_of(NSAMP + y * NS, NS), NS)
        mine = pl.ds(to * SHARE, SHARE)
        src, dst = (
            (picked.at[mine], rhs.at[:, here]),
            (zbufs[0][0], rows.at[:, there]),
            (zbufs[1][0], rows.at[:, here]),
            (None, None),
        )[kind]
        return remote(src, dst, ysend.at[kind, d - 1], yrecv.at[kind, d - 1], at(dy=d))

    for side in (0, 1):
        ocopy(side, 0, 1 - side).wait_recv()
        ocopy(side, 1, side).wait_recv()

    CHUNK = 64 * TILE

    def multiply(i, total):
        part = pl.ds(pl.multiple_of(i * CHUNK, CHUNK), CHUNK)
        return total + jnp.dot(lhs[:, part], omega_all[part], preferred_element_type=jnp.float32)

    total = lax.fori_loop(0, KMAX * TILE // CHUNK, multiply, jnp.zeros((TR * NS, TILE), jnp.float32))
    image = total.astype(BF)
    for r in range(TR):
        zbufs[1][0][r] = image[r * NS:(r + 1) * NS]

    def y_hook():
        for kind in (0, 1, 2):
            for d in (1, 3, 2):
                ycopy(kind, d).start()

    eye = lax.broadcasted_iota(jnp.int32, (TILE, TILE), 0) == lax.broadcasted_iota(
        jnp.int32, (TILE, TILE), 1
    )

    def early_hook():
        here = pl.ds(pl.multiple_of(y * NS, NS), NS)
        there = pl.ds(pl.multiple_of(NSAMP + y * NS, NS), NS)
        for r in range(TR):
            rows[r, here] = zbufs[1][0][r]
            rows[r, there] = zbufs[0][0][r]

        def keep(e, carry):
            rhs[e, here] = picked[y * SHARE + e]
            return carry

        lax.fori_loop(0, SHARE, keep, 0, unroll=8)
        for kind in (0, 1, 2):
            for d in range(1, NY):
                ycopy(kind, d).wait_recv()
        for r in range(TR):
            rows_t[r] = rows[r].T

        def start(e, carry):
            k = y * SHARE + e
            gradient = jnp.dot(rows_t[row_s[0, k], :, :NSAMP], rhs[e], preferred_element_type=jnp.float32)
            omega = omega_ref[e]
            on_diag = eye & (k < TR)
            inverse = jnp.where(on_diag, 1.0 / jnp.where(on_diag, omega, 1.0), 0.0)
            started[e] = omega - (gradient * (0.5 / NSAMP) - inverse)
            return carry

        lax.fori_loop(0, SHARE, start, 0, unroll=4)

    gather(1, (lambda: None, y_hook, lambda: None, early_hook))

    place = places[1]

    PART = SHARE // 4

    def lastcopy(d, half):
        here = pl.ds(pl.multiple_of(y * NS, NS), NS)
        return remote(
            picked_image.at[pl.ds(ys[d] * SHARE + half * PART, PART)],
            rhs_image.at[pl.ds(half * PART, PART), here],
            lsend.at[half, d - 1],
            lrecv.at[half, d - 1],
            at(dy=d),
        )

    for half in range(4):
        for d in (2, 1, 3, 0):
            for e in range(half * PART, (half + 1) * PART):
                k = ys[d] * SHARE + e
                tile = place[slot_s[0, k]]
                if d:
                    picked_image[k] = tile
                else:
                    rhs_image[e, pl.ds(pl.multiple_of(y * NS, NS), NS)] = tile
            if d:
                lastcopy(d, half).start()

    def update(e, carry):
        k = y * SHARE + e
        gradient = jnp.dot(rows_t[row_s[0, k], :, NSAMP:], rhs_image[e], preferred_element_type=jnp.float32)
        stepped = started[e] - gradient * (0.5 / NSAMP)
        shrunk = stepped - jnp.minimum(jnp.maximum(stepped, -penalty), penalty)
        proximal = jnp.where(eye & (k < TR), stepped, shrunk)
        held = jnp.where(active_s[0, k] > 0, proximal, omega_ref[e])
        out_ref[e] = jnp.where(k < count, held, 0.0)
        return carry

    def outcopy(half):
        part = pl.ds(half * PART, PART)
        return pltpu.make_async_copy(out_ref.at[part], out_hbm.at[part], lsem.at[2 + half])

    for half in range(4):
        for d in range(1, NY):
            lastcopy(d, half).wait_recv()
        lax.fori_loop(half * PART, (half + 1) * PART, update, 0, unroll=4)
        outcopy(half).start()

    for phase in (0, 1):
        for j in range(1, CHUNKS):
            zcopy(phase, j).wait_send()
        wait_all(phase).wait_send()
    wplane().wait_send()
    for i in range(1, len(AROUND)):
        wforward(i).wait_send()
    for side in (0, 1):
        for half in (0, 1):
            ocopy(side, 0, half).wait_send()
        ocopy(side, 1, side).wait_send()
    for d in range(1, NY):
        for kind in range(3):
            ycopy(kind, d).wait_send()
        for half in range(4):
            lastcopy(d, half).wait_send()
    for half in range(4):
        outcopy(half).wait()


def local(data, omega, tile_row, tile_col, tile_count, tile_active):
    vmem = pl.BlockSpec(memory_space=pltpu.VMEM)
    hbm = pl.BlockSpec(memory_space=pltpu.HBM)
    smem = pl.BlockSpec(memory_space=pltpu.SMEM)
    block = pltpu.VMEM((TR, NS, TILE), BF)
    scratch = [block] * (2 * CHUNKS)
    scratch += [pltpu.VMEM((SLOTS - LOCAL, NS, TILE), BF)] * 2
    scratch += [pltpu.VMEM((SLOTS + TR, NS, TILE), BF)] * 2
    scratch += [pltpu.VMEM(data.shape, data.dtype), pltpu.VMEM(omega.shape, omega.dtype)] + [pltpu.VMEM(omega.shape, omega.dtype)]
    scratch += [
        pltpu.VMEM((KMAX * TILE, TILE), BF),
        pltpu.VMEM((TR * NS, KMAX * TILE), BF),
        pltpu.VMEM((KMAX, NS, TILE), BF),
        pltpu.VMEM((KMAX, NS, TILE), BF),
        pltpu.VMEM((SHARE, NSAMP, TILE), BF),
        pltpu.VMEM((SHARE, NSAMP, TILE), BF),
        pltpu.VMEM((SHARE, TILE, TILE), jnp.float32),
        pltpu.VMEM((TR, 2 * NSAMP, TILE), BF),
        pltpu.VMEM((TR, TILE, 2 * NSAMP), BF),
        pltpu.VMEM((len(AROUND) * PLANE, 1, TILE), jnp.int32),
        pltpu.SMEM((len(AROUND) * PLANE, 1, TILE), jnp.int32),
        pltpu.VMEM((1, KMAX), jnp.int32),
        pltpu.SMEM((1, KMAX), jnp.int32),
    ]
    dma = pltpu.SemaphoreType.DMA
    scratch += [dma((2, CHUNKS - 1)), dma((2, CHUNKS - 1)), dma((2,)), dma((2,))]
    scratch += [dma((len(AROUND),)), dma((len(AROUND),)), dma((6,))]
    scratch += [dma((6,)), dma((6,)), dma((3, NY - 1)), dma((3, NY - 1)), dma((4, NY - 1)), dma((4, NY - 1))]
    return pl.pallas_call(
        kernel,
        out_shape=jax.ShapeDtypeStruct(omega.shape, omega.dtype),
        in_specs=[hbm, hbm, vmem, smem, smem, smem, smem],
        out_specs=hbm,
        scratch_shapes=scratch,
        compiler_params=pltpu.CompilerParams(
            collective_id=0, has_side_effects=True, vmem_limit_bytes=60 * 2**20
        ),
    )(data, omega, tile_col, tile_row, tile_col, tile_count, tile_active)


def solution(mesh):
    placed = (
        P("samp", "var"),
        P(("var", "samp"), None, None),
        P("var", None),
        P("var", None),
        P("var"),
        P("var", None),
    )
    return jax.shard_map(
        local, mesh=mesh, in_specs=placed, out_specs=P(("var", "samp"), None, None), check_vma=False
    )
```
